128 devices in a mesh: rep: 16 (over x_hi, z, core), shard: 8 (over y, x_lo).
Axes of the slice: x: 4 (x_hi: 2, x_lo: 2; x = x_hi * 2 + x_lo), y: 4, z: 4, core: 2. Of those that a mesh axis runs over, the one named last changes fastest.
Arguments:
- anchor: bfloat16 [8, 256, 3072], P('shard'), may hold values from -4 to 4
- local_params: bfloat16 [16, 8, 256, 3072], P('rep', 'shard'), may hold values from -6 to 6
- momentum: float32 [8, 256, 3072], P('shard', 'rep'), may hold values from -4 to 4
- out_grad: bfloat16 [16, 1024, 3072], P('rep', 'shard'), may hold values from -4 to 4
- pre_act: bfloat16 [16, 1024, 12288], P('rep', None, 'shard'), may hold values from -6 to 6
- down_weight: bfloat16 [16, 12288, 3072], P('rep', 'shard'), may hold values from -0.0546875 to 0.0546875
Outputs:
- new_anchor: bfloat16 [8, 256, 3072], P('shard')
- new_momentum: float32 [8, 256, 3072], P('shard', 'rep')
- pre_grad: bfloat16 [16, 1024, 12288], P('rep', None, 'shard')
- weight_grad: bfloat16 [16, 12288, 3072], P('rep', 'shard')
The draws below stay inside these ranges and needn't reach their ends.
All inputs are finite; a program needn't handle non-finite values. Where the reference program divides by a largest or mean magnitude, that divisor is 1e-20 or more.
Results may differ from the reference program's by a relative error of at most 0.0069.
Values may be sent and summed in bfloat16 or wider, within the bound.
No kernel may reach another device: no remote copies, remote signals or barrier semaphores. Data moves between devices by JAX's collectives and lax.ppermute only.
A program may use at most 128 MiB of HBM per device.

```python
import jax
import jax.numpy as jnp
from jax import lax

D = 3072
FF = 12288
BLOCK = 128
REPLICAS = 16
SHARDS = 8
SROWS = 256
TOKENS = 1024


def with_spikes(array, key, source, target, shards_of, factor):
    def block_of(dim):
        return (jnp.arange(array.shape[dim]) // (array.shape[dim] // shards_of)).reshape((-1,) + (1,) * (array.ndim - 1 - dim))

    first = jax.random.permutation(key, shards_of)[block_of(target)]
    second = (block_of(target) + shards_of // 2) % shards_of
    return jnp.where((block_of(source) == first) | (block_of(source) == second), factor * array, array)


def block_scale(stream_key, dims, pieces, least, largest):
    gain, own = 1.0, jax.random.fold_in(stream_key, 6)
    for dim, parts in pieces:
        steps = jnp.exp(jax.random.uniform(jax.random.fold_in(own, dim), (parts,), jnp.float32, least / len(pieces), largest / len(pieces)))
        gain = gain * jnp.repeat(steps, dims[dim] // parts).reshape([-1 if axis == dim else 1 for axis in range(len(dims))])
    return gain


def bell_draw(own_key, dims, width, limit, split=(), dtype=jnp.bfloat16):
    drawn = jax.random.normal(own_key, dims, jnp.float32) * width
    if len(split) > 0:
        drawn = block_scale(own_key, dims, split, -0.22, 0.18) * drawn
    return jnp.clip(drawn, min=-limit, max=limit).astype(dtype)


def bell_draw_with(key, dims, deviation, limit, shards, heavy, dtype=jnp.bfloat16):
    drawn = deviation * jax.random.normal(key, dims, jnp.float32)
    if shards:
        drawn = drawn * block_scale(key, dims, shards, -0.22, 0.18)
    return jnp.clip(with_spikes(drawn, jax.random.fold_in(key, 3), *heavy), -limit, limit).astype(dtype)


def setup_inputs(seed: int = 0) -> dict:
    key_of = jax.random.split(jax.random.key(seed), 7)
    return {
        "anchor": bell_draw(key_of[0], (SHARDS, SROWS, D), 0.5, 4.0, ((0, 8),)),
        "local_params": bell_draw_with(key_of[1], (REPLICAS, SHARDS, SROWS, D), 1.0, 6.0, ((0, 16), (1, 8)), (0, 2, 16, 2.0)),
        "momentum": bell_draw(key_of[2], (SHARDS, SROWS, D), 0.5, 4.0, ((0, 8), (1, 16)), jnp.float32),
        "out_grad": bell_draw(key_of[3], (REPLICAS, TOKENS, D), 0.5, 4.0, ((0, 16), (1, 8))),
        "pre_act": bell_draw(key_of[4], (REPLICAS, TOKENS, FF), 1.0, 6.0, ((0, 16), (2, 8))),
        "down_weight": bell_draw(key_of[5], (REPLICAS, FF, D), FF ** -0.5, 0.0546875, ((0, 16), (1, 8))),
    }


epsilon = 1e-06
outer_beta = 0.9
outer_rate = 0.7

def encode(values):
    layout = values.shape
    blocks = values.reshape(layout[:-1] + (layout[-1] // BLOCK, BLOCK))
    scales = (lax.optimization_barrier(jnp.max(jnp.abs(blocks), axis=-1)) + epsilon).astype(jnp.bfloat16)
    scales = lax.optimization_barrier(scales)
    coded = (blocks / scales.astype(jnp.float32)[..., None]).astype(jnp.bfloat16)
    coded = lax.optimization_barrier(coded)
    return (coded.reshape(layout), scales)

def decode(coded, scales):
    layout = coded.shape
    blocks = coded.astype(jnp.float32).reshape(layout[:-1] + (layout[-1] // BLOCK, BLOCK))
    return (blocks * scales.astype(jnp.float32)[..., None]).reshape(layout)

def inner_backward(operands):
    grad_rows, pre_rows, weight = operands
    hidden = jax.nn.gelu(pre_rows.astype(jnp.float32)).astype(jnp.bfloat16)
    weight_grad = lax.dot_general(hidden, grad_rows, (((0,), (0,)), ((), ())), preferred_element_type=jnp.float32)
    hidden_grad = lax.dot_general(grad_rows, weight, (((1,), (1,)), ((), ())), preferred_element_type=jnp.float32)
    _, pullback = jax.vjp(jax.nn.gelu, pre_rows.astype(jnp.float32))
    pre_grad = pullback(hidden_grad)[0].astype(jnp.bfloat16)
    return (pre_grad, weight_grad.astype(jnp.bfloat16))

def reference(anchor, local_params, momentum, out_grad, pre_act, down_weight):
    drift = anchor.astype(jnp.float32)[None] - local_params.astype(jnp.float32)
    drift_code, drift_scale = encode(drift)
    outer_grad = lax.optimization_barrier(jnp.sum(decode(drift_code, drift_scale), axis=0)) / REPLICAS
    new_momentum = outer_beta * momentum + outer_grad
    outer_step = outer_grad + outer_beta * new_momentum
    step_code, step_scale = encode(outer_step)
    new_anchor = (anchor.astype(jnp.float32) - outer_rate * decode(step_code, step_scale)).astype(jnp.bfloat16)
    pre_grad, weight_grad = lax.map(inner_backward, (out_grad, pre_act, down_weight))
    return (new_anchor, new_momentum, pre_grad, weight_grad)
```

```python
import itertools

import jax
import jax.numpy as jnp
import numpy as np
from jax import lax
from jax.experimental import pallas as pl
from jax.experimental.pallas import tpu as pltpu
from jax.sharding import PartitionSpec as P

BLOCK = 128
D = 3072
FF = 1536
CHUNK = 128
ROWS = 16

epsilon = 1e-06
outer_beta = 0.9
outer_rate = 0.7

AXES = ("rep", "shard")
MIB = 1024 * 1024
PARTS = (48, 48, 32)


def device_index(xh, z, c, y, xl):
    return ((xh % 2 * 4 + z % 4) * 2 + c % 2) * 8 + y % 4 * 2 + xl % 2


def every_device():
    return itertools.product(range(2), range(4), range(2), range(4), range(2))


def shift(array, xh=0, z=0, c=0, y=0, xl=0):
    pairs = [
        (device_index(*at), device_index(at[0] + xh, at[1] + z, at[2] + c, at[3] + y, at[4] + xl))
        for at in every_device()
    ]
    return lax.ppermute(array, AXES, pairs)


def place_table():
    table = np.zeros((128, 12), np.int32)
    for at in every_device():
        xh, z, c, y, xl = at
        order = [(y, xl), (y - 1, xl), (y + 1, xl), (y, 1 - xl), (y + 1, 1 - xl), (y - 1, 1 - xl), (y + 2, xl), (y + 2, 1 - xl)]
        table[device_index(*at)] = [a % 4 * 2 + b for a, b in order] + [xh, z, c, (xh * 4 + z) * 2 + c]
    return table


def code_and_decode(values):
    scale = (jnp.max(jnp.abs(values), axis=-1, keepdims=True) + epsilon).astype(jnp.bfloat16).astype(jnp.float32)
    return (values / scale).astype(jnp.bfloat16).astype(jnp.float32) * scale


def drift_kernel(place, anchor, local, keep, send):
    xh, c = place[8], place[10]
    for side, out in ((1, send), (0, keep)):
        for dxh in range(2):
            rows = pl.ds(pl.multiple_of((c ^ side) * ROWS, ROWS), ROWS)
            at = xh ^ dxh
            for j in range(D // BLOCK):
                cols = pl.ds(j * BLOCK, BLOCK)
                a = anchor[at, 0, rows, cols].astype(jnp.float32)
                l = local[at, 0, rows, cols].astype(jnp.float32)
                out[0, dxh, :, cols] = code_and_decode(a - l)


def drift(place, anchor, local):
    block = pl.BlockSpec((2, 1, 2 * ROWS, D), lambda i, s: (0, (s[9] + i) % 4, 0, 0))
    out = pl.BlockSpec((1, 2, ROWS, D), lambda i, s: (i, 0, 0, 0))
    shape = jax.ShapeDtypeStruct((4, 2, ROWS, D), jnp.float32)
    return pl.pallas_call(
        drift_kernel,
        out_shape=(shape, shape),
        grid_spec=pltpu.PrefetchScalarGridSpec(
            num_scalar_prefetch=1, grid=(4,), in_specs=[block, block], out_specs=[out, out]
        ),
        compiler_params=pltpu.CompilerParams(vmem_limit_bytes=16 * MIB),
        cost_estimate=pl.CostEstimate(flops=20_000_000, bytes_accessed=9_500_000, transcendentals=0),
        name="drift",
    )(place, anchor.reshape(2, 4, 2 * ROWS, D), local.reshape(2, 4, 2 * ROWS, D))


def step_kernel(place, kept, came, anchor, momentum, new_momentum, new_rows):
    for j in range(D // BLOCK):
        cols = pl.ds(j * BLOCK, BLOCK)
        outer_grad = (kept[:, cols] + came[:, cols]) / 16.0
        moved = outer_beta * momentum[:, cols] + outer_grad
        new_momentum[:, cols] = moved
        step = code_and_decode(outer_grad + outer_beta * moved)
        new_rows[:, cols] = (anchor[0, :, cols].astype(jnp.float32) - outer_rate * step).astype(jnp.bfloat16)


def outer_step(place, kept, came, anchor, momentum):
    whole = pl.BlockSpec((ROWS, D), lambda i, s: (0, 0))
    return pl.pallas_call(
        step_kernel,
        out_shape=(jax.ShapeDtypeStruct((ROWS, D), jnp.float32), jax.ShapeDtypeStruct((ROWS, D), jnp.bfloat16)),
        grid_spec=pltpu.PrefetchScalarGridSpec(
            num_scalar_prefetch=1,
            grid=(1,),
            in_specs=[whole, whole, pl.BlockSpec((1, ROWS, D), lambda i, s: (s[11], 0, 0)), whole],
            out_specs=[whole, whole],
        ),
        compiler_params=pltpu.CompilerParams(vmem_limit_bytes=8 * MIB),
        cost_estimate=pl.CostEstimate(flops=2_000_000, bytes_accessed=1_000_000, transcendentals=0),
        name="outer_step",
    )(place, kept, came, anchor.reshape(16, ROWS, D), momentum)


def place_kernel(place, mine, other, out):
    xh, c = place[8], place[10]
    for side, source in ((0, mine), (1, other)):
        for dxh in range(2):
            rows = pl.ds(pl.multiple_of((c ^ side) * ROWS, ROWS), ROWS)
            out[xh ^ dxh, 0, rows, :] = source[0, dxh]


def place_rows(place, mine, other):
    source = pl.BlockSpec((1, 2, ROWS, D), lambda i, s: (i, 0, 0, 0))
    return pl.pallas_call(
        place_kernel,
        out_shape=jax.ShapeDtypeStruct((2, 4, 2 * ROWS, D), jnp.bfloat16),
        grid_spec=pltpu.PrefetchScalarGridSpec(
            num_scalar_prefetch=1,
            grid=(4,),
            in_specs=[source, source],
            out_specs=pl.BlockSpec((2, 1, 2 * ROWS, D), lambda i, s: (0, (s[9] + i) % 4, 0, 0)),
        ),
        compiler_params=pltpu.CompilerParams(vmem_limit_bytes=8 * MIB),
        cost_estimate=pl.CostEstimate(flops=0, bytes_accessed=3_200_000, transcendentals=0),
        name="place_rows",
    )(place, mine, other)


ROOT = 0.7978845608028654
CUBIC = 0.044715


def gelu_kernel(place, pre, hidden_t, slope):
    x = pre[0].astype(jnp.float32)
    square = x * x
    t = jnp.tanh(ROOT * (x + CUBIC * (square * x)))
    half = 0.5 * (1.0 + t)
    hidden_t[...] = (x * half).astype(jnp.bfloat16).T
    slope[0] = half + 0.5 * x * (1.0 - t * t) * (ROOT * (1.0 + (3.0 * CUBIC) * square))


def gelu(place, pre_act):
    return pl.pallas_call(
        gelu_kernel,
        out_shape=(
            jax.ShapeDtypeStruct((FF, 8 * CHUNK), jnp.bfloat16),
            jax.ShapeDtypeStruct((8, CHUNK, FF), jnp.float32),
        ),
        grid_spec=pltpu.PrefetchScalarGridSpec(
            num_scalar_prefetch=1,
            grid=(8,),
            in_specs=[pl.BlockSpec((1, CHUNK, FF), lambda i, s: (s[i], 0, 0))],
            out_specs=[
                pl.BlockSpec((FF, CHUNK), lambda i, s: (0, i)),
                pl.BlockSpec((1, CHUNK, FF), lambda i, s: (i, 0, 0)),
            ],
        ),
        compiler_params=pltpu.CompilerParams(vmem_limit_bytes=16 * MIB),
        cost_estimate=pl.CostEstimate(flops=30_000_000, bytes_accessed=12_600_000, transcendentals=1_572_864),
        name="gelu",
    )(place, pre_act.reshape(8, CHUNK, FF))


def gathered(refs):
    return jnp.concatenate([ref[...] for ref in refs], axis=0) if len(refs) > 1 else refs[0][...]


def backward_kernel(plan, place, *refs):
    n_grad, hidden, weight, base, begun, size = plan
    refs = list(refs)
    grads, refs = refs[:n_grad], refs[n_grad:]
    w, refs = refs[0], refs[1:]
    slopes, refs = refs[: len(hidden)], refs[len(hidden) :]
    hts, refs = refs[: len(weight)], refs[len(weight) :]
    if base:
        acc, refs = refs[0], refs[1:]
    if begun:
        refs = refs[1:]
    if weight:
        out, refs = refs[0], refs[1:]
    pre_grad, staged, sems = refs
    j, steps = pl.program_id(0), pl.num_programs(0)
    slot = j % 2

    def copies(step, slot):
        cols = pl.ds(pl.multiple_of(step * size, size), size)
        return [
            pltpu.make_async_copy(
                staged.at[slot, pl.ds(k * CHUNK, CHUNK)], pre_grad.at[place[p], :, cols], sems.at[slot, k]
            )
            for k, p in enumerate(hidden)
        ]

    @pl.when(j >= 2)
    def _():
        for copy in copies(j - 2, slot):
            copy.wait()

    rows = gathered(grads)
    first = rows[rows.shape[0] - len(hidden) * CHUNK :]
    back = lax.dot_general(first, w[...], (((1,), (1,)), ((), ())), preferred_element_type=jnp.float32)
    for k in range(len(hidden)):
        block = pl.ds(k * CHUNK, CHUNK)
        staged[slot, block] = (back[k * CHUNK : (k + 1) * CHUNK] * slopes[k][0]).astype(jnp.bfloat16)
    for copy in copies(j, slot):
        copy.start()
    if weight:
        left = jnp.concatenate([ref[...] for ref in hts], axis=1)
        total = jnp.dot(left, rows, preferred_element_type=jnp.float32)
        if base:
            total = total + acc[...].astype(jnp.float32)
        out[...] = total.astype(out.dtype)

    @pl.when(j == steps - 1)
    def _():
        for copy in copies(j - 1, 1 - slot) + copies(j, slot):
            copy.wait()


def backward(place, grads, w, slope, hidden_t, pre_grad, hidden, weight=(), base=None, out_dtype=jnp.bfloat16, size=256):
    steps = FF // size
    in_specs = [pl.BlockSpec(g.shape, lambda j, s: (0, 0)) for g in grads]
    in_specs.append(pl.BlockSpec((size, D), lambda j, s: (j, 0)))
    in_specs += [pl.BlockSpec((1, CHUNK, size), lambda j, s, p=p: (p, 0, j)) for p in hidden]
    in_specs += [pl.BlockSpec((size, CHUNK), lambda j, s, p=p: (j, p)) for p in weight]
    operands = list(grads) + [w] + [slope] * len(hidden) + [hidden_t] * len(weight)
    if base is not None:
        in_specs.append(pl.BlockSpec((size, D), lambda j, s: (j, 0)))
        operands.append(base)
    aliases = {}
    if pre_grad is not None:
        in_specs.append(pl.BlockSpec(memory_space=pl.ANY))
        operands.append(pre_grad)
        aliases = {len(operands): int(bool(weight))}
    out_specs, out_shape = [], []
    if weight:
        out_specs.append(pl.BlockSpec((size, D), lambda j, s: (j, 0)))
        out_shape.append(jax.ShapeDtypeStruct((FF, D), out_dtype))
    out_specs.append(pl.BlockSpec(memory_space=pl.ANY))
    out_shape.append(jax.ShapeDtypeStruct((8, CHUNK, FF), jnp.bfloat16))
    plan = (len(grads), tuple(hidden), tuple(weight), base is not None, pre_grad is not None, size)
    flops = 2 * FF * D * CHUNK * (len(hidden) + len(weight))

    def kernel(place, *refs):
        backward_kernel(plan, place, *refs)

    return pl.pallas_call(
        kernel,
        out_shape=tuple(out_shape),
        grid_spec=pltpu.PrefetchScalarGridSpec(
            num_scalar_prefetch=1,
            grid=(steps,),
            in_specs=in_specs,
            out_specs=out_specs,
            scratch_shapes=[
                pltpu.VMEM((2, len(hidden) * CHUNK, size), jnp.bfloat16),
                pltpu.SemaphoreType.DMA((2, len(hidden))),
            ],
        ),
        input_output_aliases=aliases,
        compiler_params=pltpu.CompilerParams(vmem_limit_bytes=40 * MIB),
        cost_estimate=pl.CostEstimate(
            flops=flops, bytes_accessed=FF * D * 2 * (1 + 2 * bool(weight)), transcendentals=0
        ),
        name="backward",
    )(place, *operands)


def shards(anchor, local_params, momentum, out_grad, pre_act, down_weight):
    anchor, local, momentum = anchor[0], local_params[0, 0], momentum[0]
    own, pre, w = out_grad[0], pre_act[0], down_weight[0]
    number = lax.axis_index("rep") * 8 + lax.axis_index("shard")
    place = lax.dynamic_index_in_dim(jnp.asarray(place_table()), number, keepdims=False)

    ym = shift(own, y=1)
    yp = shift(own, y=-1)
    x = shift(own, xl=1)

    keep, send = drift(place, anchor, local)
    halves = keep + shift(send, c=1)
    sums = halves[0] + shift(halves[1], z=1) + shift(halves[2], z=2) + shift(halves[3], z=3)
    came = shift(sums[1], xh=1)
    new_momentum, rows = outer_step(place, sums[0], came, anchor, momentum)

    hidden_t, slope = gelu(place, pre)

    xyp = shift(yp, xl=1)
    xym = shift(x, y=1)
    y2 = shift(yp, y=-1)
    partial, pre_grad = backward(
        place, [own, ym, yp, x], w, slope, hidden_t, None, hidden=(0, 1, 2, 3), weight=(0, 1, 2, 3)
    )
    a, b, _ = PARTS
    last = [
        shift(y2[:a], xl=1),
        shift(xym[a : a + b], y=1),
        shift(xyp[a + b :], y=-1),
    ]
    (pre_grad,) = backward(place, [xyp, xym, y2], w, slope, hidden_t, pre_grad, hidden=(4, 5, 6))
    weight_grad, pre_grad = backward(
        place,
        [xyp, xym, y2, *last],
        w,
        slope,
        hidden_t,
        pre_grad,
        hidden=(7,),
        weight=(4, 5, 6, 7),
        base=partial,
    )

    pair = jnp.stack([rows, shift(rows, xh=1)])
    mine = jnp.stack([pair, shift(pair, z=3), shift(pair, z=2), shift(pair, z=1)])
    new_anchor = place_rows(place, mine, shift(mine, c=1))
    return (
        new_anchor.reshape(1, 256, D),
        new_momentum[None],
        pre_grad.reshape(1, 8 * CHUNK, FF),
        weight_grad[None],
    )


def solution(mesh):
    return jax.shard_map(
        shards,
        mesh=mesh,
        in_specs=(
            P("shard", None, None),
            P("rep", "shard", None, None),
            P("shard", "rep", None),
            P("rep", "shard", None),
            P("rep", None, "shard"),
            P("rep", "shard", None),
        ),
        out_specs=(
            P("shard", None, None),
            P("shard", "rep", None),
            P("rep", None, "shard"),
            P("rep", "shard", None),
        ),
        check_vma=False,
    )
```

```python
import itertools

import jax
import jax.numpy as jnp
import numpy as np
from jax import lax
from jax.experimental import pallas as pl
from jax.experimental.pallas import tpu as pltpu
from jax.sharding import PartitionSpec as P

BLOCK = 128
D = 3072
FF = 1536
CHUNK = 128
ROWS = 16

epsilon = 1e-06
outer_beta = 0.9
outer_rate = 0.7

AXES = ("rep", "shard")
MIB = 1024 * 1024
PER_US = 1_000_000_000
VMEM = pl.BlockSpec(memory_space=pltpu.VMEM)
SMEM = pl.BlockSpec(memory_space=pltpu.SMEM)
HBM = pl.BlockSpec(memory_space=pltpu.HBM)
ANY = pl.BlockSpec(memory_space=pl.ANY)


def device_index(xh, z, c, y, xl):
    return ((xh % 2 * 4 + z % 4) * 2 + c % 2) * 8 + y % 4 * 2 + xl % 2


def every_device():
    return itertools.product(range(2), range(4), range(2), range(4), range(2))


def shift(array, xh=0, z=0, c=0, y=0, xl=0):
    pairs = []
    for at in every_device():
        step = y(at[2]) if callable(y) else y
        pairs.append((device_index(*at), device_index(at[0] + xh, at[1] + z, at[2] + c, at[3] + step, at[4] + xl)))
    return lax.ppermute(array, AXES, pairs)


def place_table():
    table = np.zeros((128, 12), np.int32)
    for at in every_device():
        xh, z, c, y, xl = at
        order = [(y, xl), (y - 1, xl), (y + 1, xl), (y, 1 - xl), (y + 1, 1 - xl), (y - 1, 1 - xl), (y + 2, xl), (y + 2, 1 - xl)]
        table[device_index(*at)] = [a % 4 * 2 + b for a, b in order] + [xh, z, c, (xh * 4 + z) * 2 + c]
    return table


def code_and_decode(values):
    scale = (jnp.max(jnp.abs(values), axis=-1, keepdims=True) + epsilon).astype(jnp.bfloat16).astype(jnp.float32)
    return (values / scale).astype(jnp.bfloat16).astype(jnp.float32) * scale


def call(kernel, place, operands, in_specs, out_shape, out_specs, scratch=(), limit=2, aliases=None, after=(), us=1.0):
    operands = [pltpu.with_memory_space_constraint(x, spec.memory_space) for x, spec in zip(operands, in_specs)]
    count, more = len(operands), len(after)
    after_specs = [HBM if x.size >= 8 * CHUNK * FF else ANY for x in after]
    after = [x if spec is ANY else pltpu.with_memory_space_constraint(x, pltpu.HBM) for x, spec in zip(after, after_specs)]

    def body(place, *refs):
        kernel(place, *refs[:count], *refs[count + more :])

    return pl.pallas_call(
        body,
        out_shape=out_shape,
        in_specs=[SMEM, *in_specs, *after_specs],
        out_specs=out_specs,
        scratch_shapes=list(scratch),
        input_output_aliases=aliases or {},
        compiler_params=pltpu.CompilerParams(vmem_limit_bytes=limit * MIB),
        cost_estimate=pl.CostEstimate(flops=int(us * PER_US), bytes_accessed=0, transcendentals=0),
        name=kernel.__name__,
    )(place, *operands, *after)


def drift_sums(place, anchor, own, other, kept, to_1, to_2, to_3, held, sems):
    xh, z, c = place[8], place[9], place[10]
    rows = pl.ds(pl.multiple_of(c * ROWS, ROWS), ROWS)
    copies = [
        [
            pltpu.make_async_copy(source.at[xh ^ dxh, (z + dz) % 4, rows], held.at[k, dz, dxh], sems.at[dz, k, dxh])
            for k, source in enumerate((anchor, own, other))
            for dxh in range(2)
        ]
        for dz in range(4)
    ]
    for copy in sum(copies, []):
        copy.start()
    for dz, out in enumerate((kept, to_1, to_2, to_3)):
        for copy in copies[dz]:
            copy.wait()

        @pl.loop(0, 2)
        def _(dxh):
            for j in range(D // BLOCK):
                cols = pl.ds(j * BLOCK, BLOCK)
                a = held[0, dz, dxh, :, cols].astype(jnp.float32)
                first = code_and_decode(a - held[1, dz, dxh, :, cols].astype(jnp.float32))
                second = code_and_decode(a - held[2, dz, dxh, :, cols].astype(jnp.float32))
                out[dxh, :, cols] = (first + second).astype(out.dtype)


def z_sums(place, kept, from_1, from_2, from_3, mine, send):
    for dxh, out in enumerate((mine, send)):
        total = kept[dxh] + from_1[dxh].astype(jnp.float32)
        total = total + from_2[dxh].astype(jnp.float32)
        out[...] = total + from_3[dxh].astype(jnp.float32)


def outer_step(place, kept, came, anchor, momentum, new_momentum, new_rows):
    rep = place[11]
    for j in range(D // BLOCK):
        cols = pl.ds(j * BLOCK, BLOCK)
        outer_grad = (kept[:, cols] + came[:, cols]) / 16.0
        moved = outer_beta * momentum[:, cols] + outer_grad
        new_momentum[:, cols] = moved
        step = code_and_decode(outer_grad + outer_beta * moved)
        new_rows[:, cols] = (anchor[rep, :, cols].astype(jnp.float32) - outer_rate * step).astype(jnp.bfloat16)


def pick(place, first, second, out):
    @pl.when(place[10] == 0)
    def _():
        out[...] = first[...]

    @pl.when(place[10] == 1)
    def _():
        out[...] = second[...]


def relay(place, *refs):
    pass


def stack(place, *refs):
    for k, ref in enumerate(refs[:-1]):
        refs[-1][k] = ref[...]


def place_rows(place, mine, other, out, sem):
    xh, z, c = place[8], place[9], place[10]
    copies = [
        pltpu.make_async_copy(
            rows.at[dz, dxh],
            out.at[xh ^ dxh, (z + dz) % 4, pl.ds(pl.multiple_of((c ^ side) * ROWS, ROWS), ROWS)],
            sem.at[8 * side + 2 * dz + dxh],
        )
        for side, rows in enumerate((mine, other))
        for dz in range(4)
        for dxh in range(2)
    ]
    for copy in copies:
        copy.start()
    for copy in copies:
        copy.wait()


ROOT = 0.7978845608028654
CUBIC = 0.044715
WIDTH = 256


def gelu(first):
    def kernel(place, pre, hidden_t, slope, held, sems):
        copies = [pltpu.make_async_copy(pre.at[place[first + i]], held.at[i], sems.at[i]) for i in range(4)]
        for copy in copies:
            copy.start()
        for i, copy in enumerate(copies):
            copy.wait()
            here = slice(i * CHUNK, (i + 1) * CHUNK)
            for j in range(FF // WIDTH):
                cols = slice(j * WIDTH, (j + 1) * WIDTH)
                x = held[i, :, cols].astype(jnp.float32)
                square = x * x
                t = jnp.tanh(ROOT * (x + CUBIC * (square * x)))
                half = 0.5 * (1.0 + t)
                hidden_t[cols, here] = (x * half).astype(jnp.bfloat16).T
                slope[here, cols] = half + 0.5 * x * (1.0 - t * t) * (ROOT * (1.0 + (3.0 * CUBIC) * square))

    kernel.__name__ = f"gelu_{first}"
    return kernel


def pre_grads(place, rows, w, slope, staged, pre_grad, sems, first):
    copies = []
    for j in range(FF // WIDTH):
        cols = slice(j * WIDTH, (j + 1) * WIDTH)
        if rows.shape[0] > CHUNK:
            back = lax.dot_general(rows[...], w[cols], (((1,), (1,)), ((), ())), preferred_element_type=jnp.float32)
        else:
            back = lax.dot_general(w[cols], rows[...], (((1,), (1,)), ((), ())), preferred_element_type=jnp.float32).T
        staged[:, cols] = (back * slope[:, cols]).astype(jnp.bfloat16)
        if j % 2:
            cols = pl.ds((j - 1) * WIDTH, 2 * WIDTH)
            for k in range(rows.shape[0] // CHUNK):
                source = staged.at[pl.ds(k * CHUNK, CHUNK), cols]
                copy = pltpu.make_async_copy(source, pre_grad.at[place[first + k], :, cols], sems.at[j // 2, k])
                copy.start()
                copies.append(copy)
    return copies


def join(chunks, rows):
    at = 0
    for chunk in chunks:
        rows[at : at + chunk.shape[0]] = chunk[...]
        at += chunk.shape[0]


def hidden_grad(first, count, again):
    def kernel(place, *refs):
        chunks, (w, slope) = refs[:count], refs[count : count + 2]
        pre_grad, staged, sems = refs[-3:]
        rows = chunks[0]
        if count > 1:
            rows = refs[-4 - again]
            join(chunks, rows)
        if again:
            refs[-4][...] = chunks[-1][...]
        at = first % 4 * CHUNK
        for copy in pre_grads(place, rows, w, slope.at[at : at + count * CHUNK], staged, pre_grad, sems, first):
            copy.wait()

    kernel.__name__ = f"hidden_grad_{first}"
    return kernel


def run_hidden_grad(place, first, chunks, w, slope, pre_grad=None, again=False, after=()):
    count = len(chunks)
    operands, specs = [*chunks, w, slope], [VMEM] * (count + 2)
    out_shape = [pltpu.VMEM((count * CHUNK, D), jnp.bfloat16)] * (count > 1) + [pltpu.VMEM((CHUNK, D), jnp.bfloat16)] * again
    aliases = {}
    if pre_grad is not None:
        operands, specs = operands + [pre_grad], specs + [HBM]
        aliases = {len(operands): len(out_shape)}
    return call(
        hidden_grad(first, count, again),
        place,
        operands,
        specs,
        (*out_shape, pltpu.HBM((8, CHUNK, FF), jnp.bfloat16)),
        (*[VMEM] * len(out_shape), HBM),
        [pltpu.VMEM((count * CHUNK, FF), jnp.bfloat16), pltpu.SemaphoreType.DMA((FF // WIDTH // 2, count))],
        limit=8,
        aliases=aliases,
        after=after,
        us=1.5 + 1.3 * count,
    )


WIDE = 512


def weight_grad_first(place, rows, hidden_t, partial, token):
    token[...] = jnp.zeros_like(token)
    for j in range(D // WIDE):
        cols = slice(j * WIDE, (j + 1) * WIDE)
        partial[:, cols] = jnp.dot(hidden_t[...], rows[:, cols], preferred_element_type=jnp.float32).astype(jnp.bfloat16)


TALL = 512


def weight_grad_last(place, most, chunk, hidden_t, partial, weight_grad, rows, block, sems):
    join((most, chunk), rows)
    stored = []
    for i in range(FF // TALL):
        here = slice(i * TALL, (i + 1) * TALL)
        if i >= 2:
            stored[i - 2].wait()
        for j in range(D // WIDE):
            cols = slice(j * WIDE, (j + 1) * WIDE)
            total = jnp.dot(hidden_t[here], rows[:, cols], preferred_element_type=jnp.float32)
            block[i % 2, :, cols] = (partial[here, cols].astype(jnp.float32) + total).astype(jnp.bfloat16)
        store = pltpu.make_async_copy(block.at[i % 2], weight_grad.at[here], sems.at[i % 2])
        store.start()
        stored.append(store)
    for store in stored[-2:]:
        store.wait()


def shards(anchor, local_params, momentum, out_grad, pre_act, down_weight):
    anchor, local, momentum = anchor[0], local_params[0, 0], momentum[0]
    own, pre, w = out_grad[0], pre_act[0], down_weight[0]
    number = lax.axis_index("rep") * 8 + lax.axis_index("shard")
    place = lax.dynamic_index_in_dim(jnp.asarray(place_table()), number, keepdims=False)
    f32, bf16 = jnp.float32, jnp.bfloat16

    ym = shift(own, y=1)
    yp = shift(own, y=-1)
    x = shift(own, xl=1)

    view = (2, 4, 2 * ROWS, D)
    local = local.reshape(view)
    pair = pltpu.VMEM((2, ROWS, D), bf16)
    ht_0, slope_0 = call(
        gelu(0),
        place,
        [pre.reshape(8, CHUNK, FF)],
        [HBM],
        (pltpu.VMEM((FF, 4 * CHUNK), bf16), pltpu.VMEM((4 * CHUNK, FF), f32)),
        (VMEM,) * 2,
        [pltpu.VMEM((4, CHUNK, FF), bf16), pltpu.SemaphoreType.DMA((4,))],
        limit=6,
        us=2.8,
        after=(),
    )
    kept, to_1, to_2, to_3 = call(
        drift_sums,
        place,
        [anchor.reshape(view), local, shift(local, c=1)],
        [HBM] * 3,
        (pltpu.VMEM((2, ROWS, D), f32), pair, pair, pair),
        (VMEM,) * 4,
        [pltpu.VMEM((3, 4, 2, ROWS, D), bf16), pltpu.SemaphoreType.DMA((4, 3, 2))],
        limit=4,
        us=3.0,
        after=[slope_0],
    )
    from_z = [shift(to_1, z=1), shift(to_2, z=2), shift(to_3, z=3)]
    mine, send = call(
        z_sums,
        place,
        [kept, *from_z],
        [VMEM] * 4,
        (pltpu.VMEM((ROWS, D), f32),) * 2,
        (VMEM,) * 2,
        after=(),
        us=0.6,
    )
    came = shift(send, xh=1)

    yp, x = call(
        relay,
        place,
        [yp, x],
        [VMEM] * 2,
        (pltpu.VMEM((CHUNK, D), bf16),) * 2,
        (VMEM,) * 2,
        aliases={1: 0, 2: 1},
        us=0.1,
        after=[mine],
    )
    rows_0, pre_grad = run_hidden_grad(place, 0, [own, ym, yp, x], w, slope_0, after=[mine])
    xyp = shift(yp, xl=1)
    xym = shift(x, y=1)
    y2 = shift(yp, y=-1)
    partial, token = call(
        weight_grad_first,
        place,
        [rows_0, ht_0],
        [VMEM] * 2,
        (pltpu.VMEM((FF, D), bf16), pltpu.VMEM((8, BLOCK), f32)),
        (VMEM,) * 2,
        limit=4,
        after=(),
        us=5.6,
    )
    ht_4, slope_4 = call(
        gelu(4),
        place,
        [pre.reshape(8, CHUNK, FF)],
        [HBM],
        (pltpu.VMEM((FF, 4 * CHUNK), bf16), pltpu.VMEM((4 * CHUNK, FF), f32)),
        (VMEM,) * 2,
        [pltpu.VMEM((4, CHUNK, FF), bf16), pltpu.SemaphoreType.DMA((4,))],
        limit=6,
        us=2.8,
        after=[token],
    )
    passed = call(
        pick, place, [xym, xyp], [VMEM] * 2, pltpu.VMEM((CHUNK, D), bf16), VMEM, us=0.4, after=[slope_4]
    )
    x2 = shift(passed, y=lambda c: 1 - 2 * c)
    new_momentum, rows = call(
        outer_step,
        place,
        [mine, came, anchor.reshape(16, ROWS, D), momentum],
        [VMEM] * 4,
        (jax.ShapeDtypeStruct((ROWS, D), f32), pltpu.VMEM((ROWS, D), bf16)),
        (VMEM,) * 2,
        after=[slope_4],
        us=0.7,
    )
    near = shift(rows, xh=1)
    rows_4, pre_grad = run_hidden_grad(place, 4, [xyp, xym, y2], w, slope_4, pre_grad, after=[rows])

    pair = call(
        stack, place, [rows, near], [VMEM] * 2, pltpu.VMEM((2, ROWS, D), bf16), VMEM, us=0.4, after=[rows_4]
    )
    pairs = [pair, shift(pair, z=3), shift(pair, z=2), shift(pair, z=1)]
    (pre_grad,) = run_hidden_grad(place, 7, [x2], w, slope_4, pre_grad, after=[pair])
    mine = call(stack, place, pairs, [VMEM] * 4, pltpu.VMEM((4, 2, ROWS, D), bf16), VMEM, us=0.8, after=[pre_grad])
    other = shift(mine, c=1)
    weight_grad = call(
        weight_grad_last,
        place,
        [rows_4, x2, ht_4, partial],
        [VMEM] * 4,
        pltpu.HBM((FF, D), bf16),
        HBM,
        [pltpu.VMEM((4 * CHUNK, D), bf16), pltpu.VMEM((2, TALL, D), bf16), pltpu.SemaphoreType.DMA((2,))],
        limit=13,
        us=8.0,
        after=[mine],
    )
    new_anchor = call(
        place_rows,
        place,
        [mine, other],
        [VMEM] * 2,
        pltpu.HBM(view, bf16),
        HBM,
        [pltpu.SemaphoreType.DMA((16,))],
        us=1.5,
        after=[weight_grad],
    )
    return (
        new_anchor.reshape(1, 256, D),
        new_momentum[None],
        pre_grad.reshape(1, 8 * CHUNK, FF),
        weight_grad[None],
    )


def solution(mesh):
    return jax.shard_map(
        shards,
        mesh=mesh,
        in_specs=(
            P("shard", None, None),
            P("rep", "shard", None, None),
            P("shard", "rep", None),
            P("rep", "shard", None),
            P("rep", None, "shard"),
            P("rep", "shard", None),
        ),
        out_specs=(
            P("shard", None, None),
            P("shard", "rep", None),
            P("rep", None, "shard"),
            P("rep", "shard", None),
        ),
        check_vma=False,
    )
```

```python
import itertools

import jax
import jax.numpy as jnp
import numpy as np
from jax import lax
from jax.experimental import pallas as pl
from jax.experimental.pallas import tpu as pltpu
from jax.sharding import PartitionSpec as P

BLOCK = 128
D = 3072
FF = 1536
CHUNK = 128
ROWS = 16

epsilon = 1e-06
outer_beta = 0.9
outer_rate = 0.7

AXES = ("rep", "shard")
MIB = 1024 * 1024
PER_US = 1_000_000_000
VMEM = pl.BlockSpec(memory_space=pltpu.VMEM)
SMEM = pl.BlockSpec(memory_space=pltpu.SMEM)
HBM = pl.BlockSpec(memory_space=pltpu.HBM)
ANY = pl.BlockSpec(memory_space=pl.ANY)


def device_index(xh, z, c, y, xl):
    return ((xh % 2 * 4 + z % 4) * 2 + c % 2) * 8 + y % 4 * 2 + xl % 2


def every_device():
    return itertools.product(range(2), range(4), range(2), range(4), range(2))


def shift(array, xh=0, z=0, c=0, y=0, xl=0):
    pairs = []
    for at in every_device():
        step = y(at[2]) if callable(y) else y
        pairs.append((device_index(*at), device_index(at[0] + xh, at[1] + z, at[2] + c, at[3] + step, at[4] + xl)))
    return lax.ppermute(array, AXES, pairs)


def place_table():
    table = np.zeros((128, 12), np.int32)
    for at in every_device():
        xh, z, c, y, xl = at
        order = [(y, xl), (y - 1, xl), (y + 1, xl), (y, 1 - xl), (y + 1, 1 - xl), (y - 1, 1 - xl), (y + 2, xl), (y + 2, 1 - xl)]
        table[device_index(*at)] = [a % 4 * 2 + b for a, b in order] + [xh, z, c, (xh * 4 + z) * 2 + c]
    return table


def code_and_decode(values):
    scale = (jnp.max(jnp.abs(values), axis=-1, keepdims=True) + epsilon).astype(jnp.bfloat16).astype(jnp.float32)
    return (values / scale).astype(jnp.bfloat16).astype(jnp.float32) * scale


def call(kernel, place, operands, in_specs, out_shape, out_specs, scratch=(), limit=2, aliases=None, after=(), us=1.0):
    operands = [pltpu.with_memory_space_constraint(x, spec.memory_space) for x, spec in zip(operands, in_specs)]
    count, more = len(operands), len(after)
    after_specs = [HBM if x.size >= 8 * CHUNK * FF else ANY for x in after]
    after = [x if spec is ANY else pltpu.with_memory_space_constraint(x, pltpu.HBM) for x, spec in zip(after, after_specs)]

    def body(place, *refs):
        kernel(place, *refs[:count], *refs[count + more :])

    return pl.pallas_call(
        body,
        out_shape=out_shape,
        in_specs=[SMEM, *in_specs, *after_specs],
        out_specs=out_specs,
        scratch_shapes=list(scratch),
        input_output_aliases=aliases or {},
        compiler_params=pltpu.CompilerParams(vmem_limit_bytes=limit * MIB),
        cost_estimate=pl.CostEstimate(flops=int(us * PER_US), bytes_accessed=0, transcendentals=0),
        name=kernel.__name__,
    )(place, *operands, *after)


def drift_sums(place, anchor, own, other, kept, to_1, to_2, to_3, held, sems):
    xh, z, c = place[8], place[9], place[10]
    rows = pl.ds(pl.multiple_of(c * ROWS, ROWS), ROWS)
    copies = [
        [
            pltpu.make_async_copy(source.at[xh ^ dxh, (z + dz) % 4, rows], held.at[k, dz, dxh], sems.at[dz, k, dxh])
            for k, source in enumerate((anchor, own, other))
            for dxh in range(2)
        ]
        for dz in range(4)
    ]
    for copy in sum(copies, []):
        copy.start()
    for dz, out in enumerate((kept, to_1, to_2, to_3)):
        for copy in copies[dz]:
            copy.wait()

        @pl.loop(0, 2)
        def _(dxh):
            for j in range(D // BLOCK):
                cols = pl.ds(j * BLOCK, BLOCK)
                a = held[0, dz, dxh, :, cols].astype(jnp.float32)
                first = code_and_decode(a - held[1, dz, dxh, :, cols].astype(jnp.float32))
                second = code_and_decode(a - held[2, dz, dxh, :, cols].astype(jnp.float32))
                out[dxh, :, cols] = (first + second).astype(out.dtype)


def z_sums(place, kept, from_1, from_2, from_3, mine, send):
    for dxh, out in enumerate((mine, send)):
        total = kept[dxh] + from_1[dxh].astype(jnp.float32)
        total = total + from_2[dxh].astype(jnp.float32)
        out[...] = total + from_3[dxh].astype(jnp.float32)


def outer_step(place, kept, came, anchor, momentum, new_momentum, new_rows):
    rep = place[11]
    for j in range(D // BLOCK):
        cols = pl.ds(j * BLOCK, BLOCK)
        outer_grad = (kept[:, cols] + came[:, cols]) / 16.0
        moved = outer_beta * momentum[:, cols] + outer_grad
        new_momentum[:, cols] = moved
        step = code_and_decode(outer_grad + outer_beta * moved)
        new_rows[:, cols] = (anchor[rep, :, cols].astype(jnp.float32) - outer_rate * step).astype(jnp.bfloat16)


def pick(place, first, second, out):
    @pl.when(place[10] == 0)
    def _():
        out[...] = first[...]

    @pl.when(place[10] == 1)
    def _():
        out[...] = second[...]


def relay(place, *refs):
    pass


def stack(place, *refs):
    for k, ref in enumerate(refs[:-1]):
        refs[-1][k] = ref[...]


def place_rows(place, mine, other, out, sem):
    xh, z, c = place[8], place[9], place[10]
    copies = [
        pltpu.make_async_copy(
            rows.at[dz, dxh],
            out.at[xh ^ dxh, (z + dz) % 4, pl.ds(pl.multiple_of((c ^ side) * ROWS, ROWS), ROWS)],
            sem.at[8 * side + 2 * dz + dxh],
        )
        for side, rows in enumerate((mine, other))
        for dz in range(4)
        for dxh in range(2)
    ]
    for copy in copies:
        copy.start()
    for copy in copies:
        copy.wait()


ROOT = 0.7978845608028654
CUBIC = 0.044715
WIDTH = 256


def gelu(first):
    def kernel(place, pre, hidden_t, slope, held, sems):
        copies = [pltpu.make_async_copy(pre.at[place[first + i]], held.at[i], sems.at[i]) for i in range(4)]
        copies[0].start()
        copies[1].start()
        for i, copy in enumerate(copies):
            copy.wait()
            if i < 2:
                copies[i + 2].start()
            here = slice(i * CHUNK, (i + 1) * CHUNK)
            for j in range(FF // WIDTH):
                cols = slice(j * WIDTH, (j + 1) * WIDTH)
                x = held[i, :, cols].astype(jnp.float32)
                square = x * x
                t = jnp.tanh(ROOT * (x + CUBIC * (square * x)))
                half = 0.5 * (1.0 + t)
                hidden_t[cols, here] = (x * half).astype(jnp.bfloat16).T
                slope[here, cols] = half + 0.5 * x * (1.0 - t * t) * (ROOT * (1.0 + (3.0 * CUBIC) * square))

    kernel.__name__ = f"gelu_{first}"
    return kernel


def pre_grads(place, rows, w, slope, staged, pre_grad, sems, first):
    copies = []
    for j in range(FF // WIDTH):
        cols = slice(j * WIDTH, (j + 1) * WIDTH)
        if rows.shape[0] > CHUNK:
            back = lax.dot_general(rows[...], w[cols], (((1,), (1,)), ((), ())), preferred_element_type=jnp.float32)
        else:
            back = lax.dot_general(w[cols], rows[...], (((1,), (1,)), ((), ())), preferred_element_type=jnp.float32).T
        staged[:, cols] = (back * slope[:, cols]).astype(jnp.bfloat16)
        if j % 2:
            cols = pl.ds((j - 1) * WIDTH, 2 * WIDTH)
            for k in range(rows.shape[0] // CHUNK):
                source = staged.at[pl.ds(k * CHUNK, CHUNK), cols]
                copy = pltpu.make_async_copy(source, pre_grad.at[place[first + k], :, cols], sems.at[j // 2, k])
                copy.start()
                copies.append(copy)
    return copies


def join(chunks, rows):
    at = 0
    for chunk in chunks:
        rows[at : at + chunk.shape[0]] = chunk[...]
        at += chunk.shape[0]


def hidden_grad(first, count, again):
    def kernel(place, *refs):
        chunks, (w, slope) = refs[:count], refs[count : count + 2]
        pre_grad, staged, sems = refs[-3:]
        rows = chunks[0]
        if count > 1:
            rows = refs[-4 - again]
            join(chunks, rows)
        if again:
            refs[-4][...] = chunks[-1][...]
        at = first % 4 * CHUNK
        for copy in pre_grads(place, rows, w, slope.at[at : at + count * CHUNK], staged, pre_grad, sems, first):
            copy.wait()

    kernel.__name__ = f"hidden_grad_{first}"
    return kernel


def run_hidden_grad(place, first, chunks, w, slope, pre_grad=None, again=False, after=()):
    count = len(chunks)
    operands, specs = [*chunks, w, slope], [VMEM] * (count + 2)
    out_shape = [pltpu.VMEM((count * CHUNK, D), jnp.bfloat16)] * (count > 1) + [pltpu.VMEM((CHUNK, D), jnp.bfloat16)] * again
    aliases = {}
    if pre_grad is not None:
        operands, specs = operands + [pre_grad], specs + [HBM]
        aliases = {len(operands): len(out_shape)}
    return call(
        hidden_grad(first, count, again),
        place,
        operands,
        specs,
        (*out_shape, pltpu.HBM((8, CHUNK, FF), jnp.bfloat16)),
        (*[VMEM] * len(out_shape), HBM),
        [pltpu.VMEM((count * CHUNK, FF), jnp.bfloat16), pltpu.SemaphoreType.DMA((FF // WIDTH // 2, count))],
        limit=8,
        aliases=aliases,
        after=after,
        us=1.5 + 1.3 * count,
    )


WIDE = 512


def weight_grad_first(place, rows, hidden_t, partial, token):
    token[...] = jnp.zeros_like(token)
    for j in range(D // WIDE):
        cols = slice(j * WIDE, (j + 1) * WIDE)
        partial[:, cols] = jnp.dot(hidden_t[...], rows[:, cols], preferred_element_type=jnp.float32).astype(jnp.bfloat16)


TALL = 512


def weight_grad_last(place, most, chunk, hidden_t, partial, weight_grad, rows, block, sems):
    join((most, chunk), rows)
    stored = []
    for i in range(FF // TALL):
        here = slice(i * TALL, (i + 1) * TALL)
        if i >= 2:
            stored[i - 2].wait()
        for j in range(D // WIDE):
            cols = slice(j * WIDE, (j + 1) * WIDE)
            total = jnp.dot(hidden_t[here], rows[:, cols], preferred_element_type=jnp.float32)
            block[i % 2, :, cols] = (partial[here, cols].astype(jnp.float32) + total).astype(jnp.bfloat16)
        store = pltpu.make_async_copy(block.at[i % 2], weight_grad.at[here], sems.at[i % 2])
        store.start()
        stored.append(store)
    for store in stored[-2:]:
        store.wait()


def shards(anchor, local_params, momentum, out_grad, pre_act, down_weight):
    anchor, local, momentum = anchor[0], local_params[0, 0], momentum[0]
    own, pre, w = out_grad[0], pre_act[0], down_weight[0]
    number = lax.axis_index("rep") * 8 + lax.axis_index("shard")
    place = lax.dynamic_index_in_dim(jnp.asarray(place_table()), number, keepdims=False)
    f32, bf16 = jnp.float32, jnp.bfloat16

    ym = shift(own, y=1)
    yp = shift(own, y=-1)
    x = shift(own, xl=1)

    view = (2, 4, 2 * ROWS, D)
    local = local.reshape(view)
    pair = pltpu.VMEM((2, ROWS, D), bf16)
    ht_0, slope_0 = call(
        gelu(0),
        place,
        [pre.reshape(8, CHUNK, FF)],
        [HBM],
        (pltpu.VMEM((FF, 4 * CHUNK), bf16), pltpu.VMEM((4 * CHUNK, FF), f32)),
        (VMEM,) * 2,
        [pltpu.VMEM((4, CHUNK, FF), bf16), pltpu.SemaphoreType.DMA((4,))],
        limit=6,
        us=2.8,
        after=(),
    )
    kept, to_1, to_2, to_3 = call(
        drift_sums,
        place,
        [anchor.reshape(view), local, shift(local, c=1)],
        [HBM] * 3,
        (pltpu.VMEM((2, ROWS, D), f32), pair, pair, pair),
        (VMEM,) * 4,
        [pltpu.VMEM((3, 4, 2, ROWS, D), bf16), pltpu.SemaphoreType.DMA((4, 3, 2))],
        limit=4,
        us=3.0,
        after=[slope_0],
    )
    from_z = [shift(to_1, z=1), shift(to_2, z=2), shift(to_3, z=3)]
    mine, send = call(
        z_sums,
        place,
        [kept, *from_z],
        [VMEM] * 4,
        (pltpu.VMEM((ROWS, D), f32),) * 2,
        (VMEM,) * 2,
        after=(),
        us=0.6,
    )
    came = shift(send, xh=1)

    yp, x = call(
        relay,
        place,
        [yp, x],
        [VMEM] * 2,
        (pltpu.VMEM((CHUNK, D), bf16),) * 2,
        (VMEM,) * 2,
        aliases={1: 0, 2: 1},
        us=0.1,
        after=[kept],
    )
    rows_0, pre_grad = run_hidden_grad(place, 0, [own, ym, yp, x], w, slope_0, after=[mine])
    xyp = shift(yp, xl=1)
    xym = shift(x, y=1)
    y2 = shift(yp, y=-1)
    partial, token = call(
        weight_grad_first,
        place,
        [rows_0, ht_0],
        [VMEM] * 2,
        (pltpu.VMEM((FF, D), bf16), pltpu.VMEM((8, BLOCK), f32)),
        (VMEM,) * 2,
        limit=4,
        after=(),
        us=5.6,
    )
    ht_4, slope_4 = call(
        gelu(4),
        place,
        [pre.reshape(8, CHUNK, FF)],
        [HBM],
        (pltpu.VMEM((FF, 4 * CHUNK), bf16), pltpu.VMEM((4 * CHUNK, FF), f32)),
        (VMEM,) * 2,
        [pltpu.VMEM((4, CHUNK, FF), bf16), pltpu.SemaphoreType.DMA((4,))],
        limit=6,
        us=2.8,
        after=[token],
    )
    passed = call(
        pick, place, [xym, xyp], [VMEM] * 2, pltpu.VMEM((CHUNK, D), bf16), VMEM, us=0.4, after=[slope_4]
    )
    x2 = shift(passed, y=lambda core: 1 - 2 * core)
    new_momentum, rows = call(
        outer_step,
        place,
        [mine, came, anchor.reshape(16, ROWS, D), momentum],
        [VMEM] * 4,
        (jax.ShapeDtypeStruct((ROWS, D), f32), pltpu.VMEM((ROWS, D), bf16)),
        (VMEM,) * 2,
        after=[slope_4],
        us=0.7,
    )
    near = shift(rows, xh=1)
    rows_4, pre_grad = run_hidden_grad(place, 4, [xyp, xym, y2], w, slope_4, pre_grad, after=[rows])

    pair = call(
        stack, place, [rows, near], [VMEM] * 2, pltpu.VMEM((2, ROWS, D), bf16), VMEM, us=0.4, after=[rows_4]
    )
    pairs = [pair, shift(pair, z=3), shift(pair, z=2), shift(pair, z=1)]
    (pre_grad,) = run_hidden_grad(place, 7, [x2], w, slope_4, pre_grad, after=[pair])
    mine = call(stack, place, pairs, [VMEM] * 4, pltpu.VMEM((4, 2, ROWS, D), bf16), VMEM, us=0.8, after=[pre_grad])
    other = shift(mine, c=1)
    weight_grad = call(
        weight_grad_last,
        place,
        [rows_4, x2, ht_4, partial],
        [VMEM] * 4,
        pltpu.HBM((FF, D), bf16),
        HBM,
        [pltpu.VMEM((4 * CHUNK, D), bf16), pltpu.VMEM((2, TALL, D), bf16), pltpu.SemaphoreType.DMA((2,))],
        limit=13,
        us=8.0,
        after=[mine],
    )
    new_anchor = call(
        place_rows,
        place,
        [mine, other],
        [VMEM] * 2,
        pltpu.HBM(view, bf16),
        HBM,
        [pltpu.SemaphoreType.DMA((16,))],
        us=1.5,
        after=[weight_grad],
    )
    return (
        new_anchor.reshape(1, 256, D),
        new_momentum[None],
        pre_grad.reshape(1, 8 * CHUNK, FF),
        weight_grad[None],
    )


def solution(mesh):
    return jax.shard_map(
        shards,
        mesh=mesh,
        in_specs=(
            P("shard", None, None),
            P("rep", "shard", None, None),
            P("shard", "rep", None),
            P("rep", "shard", None),
            P("rep", None, "shard"),
            P("rep", "shard", None),
        ),
        out_specs=(
            P("shard", None, None),
            P("shard", "rep", None),
            P("rep", None, "shard"),
            P("rep", "shard", None),
        ),
        check_vma=False,
    )
```

```python
import itertools

import jax
import jax.numpy as jnp
import numpy as np
from jax import lax
from jax.experimental import pallas as pl
from jax.experimental.pallas import tpu as pltpu
from jax.sharding import PartitionSpec as P

BLOCK = 128
D = 3072
FF = 1536
CHUNK = 128
ROWS = 16

epsilon = 1e-06
outer_beta = 0.9
outer_rate = 0.7

AXES = ("rep", "shard")
MIB = 1024 * 1024
PER_US = 1_000_000_000
VMEM = pl.BlockSpec(memory_space=pltpu.VMEM)
SMEM = pl.BlockSpec(memory_space=pltpu.SMEM)
HBM = pl.BlockSpec(memory_space=pltpu.HBM)
ANY = pl.BlockSpec(memory_space=pl.ANY)


def device_index(xh, z, c, y, xl):
    return ((xh % 2 * 4 + z % 4) * 2 + c % 2) * 8 + y % 4 * 2 + xl % 2


def every_device():
    return itertools.product(range(2), range(4), range(2), range(4), range(2))


def shift(array, xh=0, z=0, c=0, y=0, xl=0):
    pairs = []
    for at in every_device():
        step = y(at[2]) if callable(y) else y
        pairs.append((device_index(*at), device_index(at[0] + xh, at[1] + z, at[2] + c, at[3] + step, at[4] + xl)))
    return lax.ppermute(array, AXES, pairs)


def place_table():
    table = np.zeros((128, 12), np.int32)
    for at in every_device():
        xh, z, c, y, xl = at
        order = [(y, xl), (y - 1, xl), (y + 1, xl), (y, 1 - xl), (y + 1, 1 - xl), (y - 1, 1 - xl), (y + 2, xl), (y + 2, 1 - xl)]
        table[device_index(*at)] = [a % 4 * 2 + b for a, b in order] + [xh, z, c, (xh * 4 + z) * 2 + c]
    return table


def code_and_decode(values):
    scale = (jnp.max(jnp.abs(values), axis=-1, keepdims=True) + epsilon).astype(jnp.bfloat16).astype(jnp.float32)
    return (values / scale).astype(jnp.bfloat16).astype(jnp.float32) * scale


def call(kernel, place, operands, in_specs, out_shape, out_specs, scratch=(), limit=2, aliases=None, after=(), us=1.0):
    operands = [pltpu.with_memory_space_constraint(x, spec.memory_space) for x, spec in zip(operands, in_specs)]
    count, more = len(operands), len(after)
    after_specs = [HBM if x.size >= 8 * CHUNK * FF else ANY for x in after]
    after = [x if spec is ANY else pltpu.with_memory_space_constraint(x, pltpu.HBM) for x, spec in zip(after, after_specs)]

    def body(place, *refs):
        kernel(place, *refs[:count], *refs[count + more :])

    return pl.pallas_call(
        body,
        out_shape=out_shape,
        in_specs=[SMEM, *in_specs, *after_specs],
        out_specs=out_specs,
        scratch_shapes=list(scratch),
        input_output_aliases=aliases or {},
        compiler_params=pltpu.CompilerParams(vmem_limit_bytes=limit * MIB),
        cost_estimate=pl.CostEstimate(flops=int(us * PER_US), bytes_accessed=0, transcendentals=0),
        name=kernel.__name__,
    )(place, *operands, *after)


def drift_sums(place, anchor, own, other, kept, to_1, to_2, to_3, held, sems):
    xh, z, c = place[8], place[9], place[10]
    rows = pl.ds(pl.multiple_of(c * ROWS, ROWS), ROWS)
    copies = [
        [
            pltpu.make_async_copy(source.at[xh ^ dxh, (z + dz) % 4, rows], held.at[k, dz, dxh], sems.at[dz, k, dxh])
            for k, source in enumerate((anchor, own, other))
            for dxh in range(2)
        ]
        for dz in range(4)
    ]
    for copy in sum(copies, []):
        copy.start()
    for dz, out in enumerate((kept, to_1, to_2, to_3)):
        for copy in copies[dz]:
            copy.wait()

        @pl.loop(0, 2)
        def _(dxh):
            for j in range(D // BLOCK):
                cols = pl.ds(j * BLOCK, BLOCK)
                a = held[0, dz, dxh, :, cols].astype(jnp.float32)
                first = code_and_decode(a - held[1, dz, dxh, :, cols].astype(jnp.float32))
                second = code_and_decode(a - held[2, dz, dxh, :, cols].astype(jnp.float32))
                out[dxh, :, cols] = (first + second).astype(out.dtype)


def z_sums(place, kept, from_1, from_2, from_3, mine, send):
    for dxh, out in enumerate((mine, send)):
        total = kept[dxh] + from_1[dxh].astype(jnp.float32)
        total = total + from_2[dxh].astype(jnp.float32)
        out[...] = total + from_3[dxh].astype(jnp.float32)


def outer_step(place, kept, came, anchor, momentum, new_momentum, new_rows):
    rep = place[11]
    for j in range(D // BLOCK):
        cols = pl.ds(j * BLOCK, BLOCK)
        outer_grad = (kept[:, cols] + came[:, cols]) / 16.0
        moved = outer_beta * momentum[:, cols] + outer_grad
        new_momentum[:, cols] = moved
        step = code_and_decode(outer_grad + outer_beta * moved)
        new_rows[:, cols] = (anchor[rep, :, cols].astype(jnp.float32) - outer_rate * step).astype(jnp.bfloat16)


def pick(place, first, second, out):
    @pl.when(place[10] == 0)
    def _():
        out[...] = first[...]

    @pl.when(place[10] == 1)
    def _():
        out[...] = second[...]


def relay(place, *refs):
    pass


def stack(place, *refs):
    for k, ref in enumerate(refs[:-1]):
        refs[-1][k] = ref[...]


def place_rows(place, mine, other, out, sem):
    xh, z, c = place[8], place[9], place[10]
    copies = [
        pltpu.make_async_copy(
            rows.at[dz, dxh],
            out.at[xh ^ dxh, (z + dz) % 4, pl.ds(pl.multiple_of((c ^ side) * ROWS, ROWS), ROWS)],
            sem.at[8 * side + 2 * dz + dxh],
        )
        for side, rows in enumerate((mine, other))
        for dz in range(4)
        for dxh in range(2)
    ]
    for copy in copies:
        copy.start()
    for copy in copies:
        copy.wait()


ROOT = 0.7978845608028654
CUBIC = 0.044715
WIDTH = 256


def gelu(first):
    def kernel(place, pre, hidden_t, slope, held, sems):
        copies = [pltpu.make_async_copy(pre.at[place[first + i]], held.at[i], sems.at[i]) for i in range(4)]
        for copy in copies:
            copy.start()
        for i, copy in enumerate(copies):
            copy.wait()
            here = slice(i * CHUNK, (i + 1) * CHUNK)
            for j in range(FF // WIDTH):
                cols = slice(j * WIDTH, (j + 1) * WIDTH)
                x = held[i, :, cols].astype(jnp.float32)
                square = x * x
                t = jnp.tanh(ROOT * (x + CUBIC * (square * x)))
                half = 0.5 * (1.0 + t)
                hidden_t[cols, here] = (x * half).astype(jnp.bfloat16).T
                slope[here, cols] = half + 0.5 * x * (1.0 - t * t) * (ROOT * (1.0 + (3.0 * CUBIC) * square))

    kernel.__name__ = f"gelu_{first}"
    return kernel


def pre_grads(place, rows, w, slope, staged, pre_grad, sems, first):
    copies = []
    for j in range(FF // WIDTH):
        cols = slice(j * WIDTH, (j + 1) * WIDTH)
        if rows.shape[0] > CHUNK:
            back = lax.dot_general(rows[...], w[cols], (((1,), (1,)), ((), ())), preferred_element_type=jnp.float32)
        else:
            back = lax.dot_general(w[cols], rows[...], (((1,), (1,)), ((), ())), preferred_element_type=jnp.float32).T
        staged[:, cols] = (back * slope[:, cols]).astype(jnp.bfloat16)
        if j % 2:
            cols = pl.ds((j - 1) * WIDTH, 2 * WIDTH)
            for k in range(rows.shape[0] // CHUNK):
                source = staged.at[pl.ds(k * CHUNK, CHUNK), cols]
                copy = pltpu.make_async_copy(source, pre_grad.at[place[first + k], :, cols], sems.at[j // 2, k])
                copy.start()
                copies.append(copy)
    return copies


def join(chunks, rows):
    at = 0
    for chunk in chunks:
        rows[at : at + chunk.shape[0]] = chunk[...]
        at += chunk.shape[0]


def hidden_grad(first, count, again):
    def kernel(place, *refs):
        chunks, (w, slope) = refs[:count], refs[count : count + 2]
        pre_grad, staged, sems = refs[-3:]
        rows = chunks[0]
        if count > 1:
            rows = refs[-4 - again]
            join(chunks, rows)
        if again:
            refs[-4][...] = chunks[-1][...]
        at = first % 4 * CHUNK
        for copy in pre_grads(place, rows, w, slope.at[at : at + count * CHUNK], staged, pre_grad, sems, first):
            copy.wait()

    kernel.__name__ = f"hidden_grad_{first}"
    return kernel


def run_hidden_grad(place, first, chunks, w, slope, pre_grad=None, again=False, after=()):
    count = len(chunks)
    operands, specs = [*chunks, w, slope], [VMEM] * (count + 2)
    out_shape = [pltpu.VMEM((count * CHUNK, D), jnp.bfloat16)] * (count > 1) + [pltpu.VMEM((CHUNK, D), jnp.bfloat16)] * again
    aliases = {}
    if pre_grad is not None:
        operands, specs = operands + [pre_grad], specs + [HBM]
        aliases = {len(operands): len(out_shape)}
    return call(
        hidden_grad(first, count, again),
        place,
        operands,
        specs,
        (*out_shape, pltpu.HBM((8, CHUNK, FF), jnp.bfloat16)),
        (*[VMEM] * len(out_shape), HBM),
        [pltpu.VMEM((count * CHUNK, FF), jnp.bfloat16), pltpu.SemaphoreType.DMA((FF // WIDTH // 2, count))],
        limit=8,
        aliases=aliases,
        after=after,
        us=1.5 + 1.3 * count,
    )


WIDE = 512


def weight_grad_first(place, rows, hidden_t, partial, token):
    token[...] = jnp.zeros_like(token)
    for j in range(D // WIDE):
        cols = slice(j * WIDE, (j + 1) * WIDE)
        partial[:, cols] = jnp.dot(hidden_t[...], rows[:, cols], preferred_element_type=jnp.float32).astype(jnp.bfloat16)


TALL = 384


def weight_grad_rows(first, rows, hidden_t, partial, weight_grad, block, sems):
    stored = []
    for i in range(2):
        here = slice(first + i * TALL, first + (i + 1) * TALL)
        for j in range(D // WIDE):
            cols = slice(j * WIDE, (j + 1) * WIDE)
            total = jnp.dot(hidden_t[here], rows[:, cols], preferred_element_type=jnp.float32)
            block[i, :, cols] = (partial[here, cols].astype(jnp.float32) + total).astype(jnp.bfloat16)
        store = pltpu.make_async_copy(block.at[i], weight_grad.at[here], sems.at[i])
        store.start()
        stored.append(store)
    for store in stored:
        store.wait()


def weight_grad_upper(place, most, chunk, hidden_t, partial, rows, weight_grad, block, sems):
    join((most, chunk), rows)
    weight_grad_rows(0, rows, hidden_t, partial, weight_grad, block, sems)


def weight_grad_lower(place, rows, hidden_t, partial, _, weight_grad, block, sems):
    weight_grad_rows(2 * TALL, rows, hidden_t, partial, weight_grad, block, sems)


def shards(anchor, local_params, momentum, out_grad, pre_act, down_weight):
    anchor, local, momentum = anchor[0], local_params[0, 0], momentum[0]
    own, pre, w = out_grad[0], pre_act[0], down_weight[0]
    number = lax.axis_index("rep") * 8 + lax.axis_index("shard")
    place = lax.dynamic_index_in_dim(jnp.asarray(place_table()), number, keepdims=False)
    f32, bf16 = jnp.float32, jnp.bfloat16

    ym = shift(own, y=1)
    yp = shift(own, y=-1)
    x = shift(own, xl=1)

    view = (2, 4, 2 * ROWS, D)
    local = local.reshape(view)
    pair = pltpu.VMEM((2, ROWS, D), bf16)
    ht_0, slope_0 = call(
        gelu(0),
        place,
        [pre.reshape(8, CHUNK, FF)],
        [HBM],
        (pltpu.VMEM((FF, 4 * CHUNK), bf16), pltpu.VMEM((4 * CHUNK, FF), f32)),
        (VMEM,) * 2,
        [pltpu.VMEM((4, CHUNK, FF), bf16), pltpu.SemaphoreType.DMA((4,))],
        limit=6,
        us=2.8,
        after=(),
    )
    kept, to_1, to_2, to_3 = call(
        drift_sums,
        place,
        [anchor.reshape(view), local, shift(local, c=1)],
        [HBM] * 3,
        (pltpu.VMEM((2, ROWS, D), f32), pair, pair, pair),
        (VMEM,) * 4,
        [pltpu.VMEM((3, 4, 2, ROWS, D), bf16), pltpu.SemaphoreType.DMA((4, 3, 2))],
        limit=4,
        us=3.0,
        after=[slope_0],
    )
    from_z = [shift(to_1, z=1), shift(to_2, z=2), shift(to_3, z=3)]
    mine, send = call(
        z_sums,
        place,
        [kept, *from_z],
        [VMEM] * 4,
        (pltpu.VMEM((ROWS, D), f32),) * 2,
        (VMEM,) * 2,
        after=(),
        us=0.6,
    )
    came = shift(send, xh=1)

    yp, x = call(
        relay,
        place,
        [yp, x],
        [VMEM] * 2,
        (pltpu.VMEM((CHUNK, D), bf16),) * 2,
        (VMEM,) * 2,
        aliases={1: 0, 2: 1},
        us=0.1,
        after=[kept],
    )
    rows_0, pre_grad = run_hidden_grad(place, 0, [own, ym, yp, x], w, slope_0, after=[mine])
    xyp = shift(yp, xl=1)
    xym = shift(x, y=1)
    y2 = shift(yp, y=-1)
    partial, token = call(
        weight_grad_first,
        place,
        [rows_0, ht_0],
        [VMEM] * 2,
        (pltpu.VMEM((FF, D), bf16), pltpu.VMEM((8, BLOCK), f32)),
        (VMEM,) * 2,
        limit=4,
        after=(),
        us=5.6,
    )
    ht_4, slope_4 = call(
        gelu(4),
        place,
        [pre.reshape(8, CHUNK, FF)],
        [HBM],
        (pltpu.VMEM((FF, 4 * CHUNK), bf16), pltpu.VMEM((4 * CHUNK, FF), f32)),
        (VMEM,) * 2,
        [pltpu.VMEM((4, CHUNK, FF), bf16), pltpu.SemaphoreType.DMA((4,))],
        limit=6,
        us=2.8,
        after=[token],
    )
    passed = call(
        pick, place, [xym, xyp], [VMEM] * 2, pltpu.VMEM((CHUNK, D), bf16), VMEM, us=0.4, after=[slope_4]
    )
    x2 = shift(passed, y=lambda core: 1 - 2 * core)
    new_momentum, rows = call(
        outer_step,
        place,
        [mine, came, anchor.reshape(16, ROWS, D), momentum],
        [VMEM] * 4,
        (jax.ShapeDtypeStruct((ROWS, D), f32), pltpu.VMEM((ROWS, D), bf16)),
        (VMEM,) * 2,
        after=[slope_4],
        us=0.7,
    )
    near = shift(rows, xh=1)
    rows_4, pre_grad = run_hidden_grad(place, 4, [xyp, xym, y2], w, slope_4, pre_grad, after=[rows])

    pair = call(
        stack, place, [rows, near], [VMEM] * 2, pltpu.VMEM((2, ROWS, D), bf16), VMEM, us=0.4, after=[rows_4]
    )
    pairs = [pair, shift(pair, z=3), shift(pair, z=2), shift(pair, z=1)]
    (pre_grad,) = run_hidden_grad(place, 7, [x2], w, slope_4, pre_grad, after=[pair])
    rows_4, upper = call(
        weight_grad_upper,
        place,
        [rows_4, x2, ht_4, partial],
        [VMEM] * 4,
        (pltpu.VMEM((4 * CHUNK, D), bf16), pltpu.HBM((FF, D), bf16)),
        (VMEM, HBM),
        [pltpu.VMEM((2, TALL, D), bf16), pltpu.SemaphoreType.DMA((2,))],
        limit=12,
        us=4.5,
        after=[pre_grad],
    )
    mine = call(stack, place, pairs, [VMEM] * 4, pltpu.VMEM((4, 2, ROWS, D), bf16), VMEM, us=0.8, after=[upper])
    other = shift(mine, c=1)
    weight_grad = call(
        weight_grad_lower,
        place,
        [rows_4, ht_4, partial, upper],
        [VMEM] * 3 + [HBM],
        pltpu.HBM((FF, D), bf16),
        HBM,
        [pltpu.VMEM((2, TALL, D), bf16), pltpu.SemaphoreType.DMA((2,))],
        limit=12,
        aliases={4: 0},
        us=4.5,
        after=[mine],
    )
    new_anchor = call(
        place_rows,
        place,
        [mine, other],
        [VMEM] * 2,
        pltpu.HBM(view, bf16),
        HBM,
        [pltpu.SemaphoreType.DMA((16,))],
        us=1.5,
        after=[weight_grad],
    )
    return (
        new_anchor.reshape(1, 256, D),
        new_momentum[None],
        pre_grad.reshape(1, 8 * CHUNK, FF),
        weight_grad[None],
    )


def solution(mesh):
    return jax.shard_map(
        shards,
        mesh=mesh,
        in_specs=(
            P("shard", None, None),
            P("rep", "shard", None, None),
            P("shard", "rep", None),
            P("rep", "shard", None),
            P("rep", None, "shard"),
            P("rep", "shard", None),
        ),
        out_specs=(
            P("shard", None, None),
            P("shard", "rep", None),
            P("rep", None, "shard"),
            P("rep", "shard", None),
        ),
        check_vma=False,
    )
```
